32 devices in a mesh: ens: 4 (over y, x), space: 8 (over z, core).
Axes of the slice: x: 2, y: 2, z: 4, core: 2. Of those that a mesh axis runs over, the one named last changes fastest.
Arguments:
- inputs: bfloat16 [8, 32, 256, 256], P('ens', None, 'space'), may hold values from -6 to 6
- target: bfloat16 [32, 256, 256], P(None, 'space'), may hold values from -6 to 6
- filter_taps: bfloat16 [3, 32, 3, 9], replicated, may hold values from -1.75 to 1.75
- lon_offset: int32 [32], replicated, may hold values from -2 to 2, as said below
- lon_width: int32 [32], replicated, may hold values from 1 to 4
- w_disco: bfloat16 [3, 256, 256], replicated, may hold values from -0.21875 to 0.21875
- w_up: bfloat16 [256, 512], replicated, may hold values from -0.375 to 0.375
- w_down: bfloat16 [512, 256], replicated, may hold values from -0.25 to 0.25
- norm_gain: float32 [256], replicated, may hold values from 0.5 to 1.5
Outputs:
- grad_input: bfloat16 [8, 32, 256, 256], P('ens', None, 'space')
- grad_disco: float32 [3, 256, 256], replicated
- grad_up: float32 [256, 512], replicated
- grad_down: float32 [512, 256], replicated
- grad_gain: float32 [256], replicated
The draws below stay inside these ranges and needn't reach their ends.
Inputs may be any that keep to these rules, and one draw needn't show every extreme that they name: |lon_offset| + lon_width <= 4 in every row; some row has offset 0 and width 4, some row offset 2, some row offset -2.
All inputs are finite; a program needn't handle non-finite values.
Results may differ from the reference program's by a relative error of at most 0.02.
Values may be sent and summed in bfloat16 or wider, within the bound.
A program may use at most 128 MiB of HBM per device.

```python
import math
import jax
import jax.numpy as jnp
from jax import lax

C = 256
FF = 512
K = 3
HALO = 4
LAT = 32
MEMBERS = 8
LON = 256


def lon_pattern(key):
    base = jax.random.fold_in(key, 11)
    first, second, third = jax.random.split(base, 3)
    offset = jax.random.randint(first, (LAT,), -2, 3, dtype=jnp.int32)
    order = jax.random.permutation(third, LAT)
    offset = offset.at[order[0]].set(0).at[order[1]].set(2).at[order[2]].set(-2)
    room = HALO - jnp.abs(offset)
    width = jax.random.randint(second, (LAT,), 1, room + 1, dtype=jnp.int32)
    width = width.at[order[0]].set(HALO)
    return (offset, width)


def draw_lon_offset(key, part):
    return lon_pattern(key)[0]


def draw_lon_width(key, part):
    return lon_pattern(key)[1]


def block_scale(own_key, extent, shards, least, high):
    loudness, own = 1.0, jax.random.fold_in(own_key, 6)
    for dim, parts in shards:
        heights = jnp.exp(jax.random.uniform(jax.random.fold_in(own, dim), (parts,), jnp.float32, least / len(shards), high / len(shards)))
        loudness = loudness * jnp.repeat(heights, extent[dim] // parts).reshape([-1 if axis == dim else 1 for axis in range(len(extent))])
    return loudness


def normal_values(own_key, dims, scale, most, cuts=(), kind=jnp.bfloat16):
    factor_of = block_scale(own_key, dims, cuts, -0.22, 0.18) if cuts else 1.0
    array = jax.random.normal(own_key, dims, jnp.float32) * scale * factor_of
    return jnp.minimum(jnp.maximum(array, -most), most).astype(kind)


def setup_inputs(seed: int = 0) -> dict:
    streams_of = jax.random.split(jax.random.key(seed), 10)
    return {
        "inputs": normal_values(streams_of[0], (MEMBERS, LAT, LON, C), 1.0, 6.0, ((0, 4), (2, 8))),
        "target": normal_values(streams_of[1], (LAT, LON, C), 1.0, 6.0, ((1, 8),)),
        "filter_taps": normal_values(streams_of[2], (K, LAT, 3, 2 * HALO + 1), 0.3, 1.75),
        "lon_offset": draw_lon_offset(jax.random.fold_in(streams_of[9], 71), 0),
        "lon_width": draw_lon_width(jax.random.fold_in(streams_of[9], 71), 0),
        "w_disco": normal_values(streams_of[5], (K, C, C), (K * C) ** -0.5, 0.21875),
        "w_up": normal_values(streams_of[6], (C, FF), C ** -0.5, 0.375),
        "w_down": normal_values(streams_of[7], (FF, C), FF ** -0.5, 0.25),
        "norm_gain": jnp.clip(1.0 + 0.1 * jax.random.normal(streams_of[8], (C,), jnp.float32), 0.5, 1.5),
    }


root_two_pi = 0.7978845608028654

def slope_abs(values):
    return values * lax.rsqrt(values * values + 0.01)

def gelu_value(preact):
    return 0.5 * preact * (1.0 + jnp.tanh(root_two_pi * (preact + 0.044715 * preact * preact * preact)))

def gelu_slope(preact):
    tangent = jnp.tanh(root_two_pi * (preact + 0.044715 * preact * preact * preact))
    return 0.5 * (1.0 + tangent) + 0.5 * preact * (1.0 - tangent * tangent) * root_two_pi * (1.0 + 3.0 * 0.044715 * preact * preact)

def masked_taps(filter_taps, lon_offset, lon_width):
    count = filter_taps.shape[3]
    reach = (count - 1) // 2
    offsets = jnp.arange(count, dtype=jnp.int32) - reach
    keep = jnp.abs(offsets[None, :] - lon_offset[:, None]) <= lon_width[:, None]
    return jnp.where(keep[None, :, None, :], filter_taps, jnp.zeros_like(filter_taps))

def stencil(member, taps):
    reach = (taps.shape[3] - 1) // 2
    rows = member.shape[0]
    padded = jnp.pad(member.astype(jnp.float32), ((1, 1), (0, 0), (0, 0)))
    total = jnp.zeros((taps.shape[0],) + member.shape, jnp.float32)
    for column in range(taps.shape[3]):
        inner = jnp.zeros_like(total)
        for shift_row in range(3):
            weights = taps[:, :, shift_row, column].astype(jnp.float32)
            inner = inner + weights[:, :, None, None] * padded[None, shift_row:shift_row + rows]
        total = total + jnp.roll(inner, reach - column, axis=2)
    return total

def adjoint(dfilt, taps):
    reach = (taps.shape[3] - 1) // 2
    rows = dfilt.shape[1]
    grads = dfilt.astype(jnp.float32)
    full = jnp.zeros((rows + 2,) + dfilt.shape[2:], jnp.float32)
    for column in range(taps.shape[3]):
        for shift_row in range(3):
            weights = taps[:, :, shift_row, column].astype(jnp.float32)
            term = lax.optimization_barrier(jnp.sum(weights[:, :, None, None] * grads, axis=0))
            full = full.at[shift_row:shift_row + rows].add(jnp.roll(term, column - reach, axis=1))
    return full[1:rows + 1]

def reference(inputs, target, filter_taps, lon_offset, lon_width, w_disco, w_up, w_down, norm_gain):
    taps = masked_taps(filter_taps, lon_offset, lon_width)
    disco_f = w_disco.astype(jnp.float32)
    up_f = w_up.astype(jnp.float32)
    down_f = w_down.astype(jnp.float32)

    def forward(member):
        filtered = stencil(member, taps).astype(jnp.bfloat16)
        hidden = jnp.einsum('kijc,kcd->ijd', filtered.astype(jnp.float32), disco_f)
        inverse = lax.rsqrt(lax.optimization_barrier(jnp.mean(hidden * hidden, axis=-1, keepdims=True)) + 1e-06)
        scaled = hidden * inverse
        normed = (scaled * norm_gain).astype(jnp.bfloat16)
        preact = jnp.einsum('ijc,cf->ijf', normed.astype(jnp.float32), up_f)
        active = gelu_value(preact).astype(jnp.bfloat16)
        output = (member.astype(jnp.float32) + jnp.einsum('ijf,fc->ijc', active.astype(jnp.float32), down_f)).astype(jnp.bfloat16)
        return (output, filtered, scaled, inverse, preact, active, normed)
    saved = lax.map(forward, inputs)
    output = saved[0]
    mine = output.astype(jnp.float32)
    miss = slope_abs(mine - target.astype(jnp.float32)[None])

    def accumulate(carry, other):
        return (carry + slope_abs(mine - other.astype(jnp.float32)[None]), None)
    spread, _ = lax.scan(accumulate, jnp.zeros_like(mine), output)
    dgrad = (miss - spread / (MEMBERS - 1)).astype(jnp.bfloat16)

    def backward(packed):
        dmember, filtered, scaled, inverse, preact, active, normed = packed
        dfloat = dmember.astype(jnp.float32)
        down_part = jnp.einsum('ijf,ijc->fc', active.astype(jnp.float32), dfloat)
        dactive = jnp.einsum('ijc,fc->ijf', dfloat, down_f).astype(jnp.bfloat16)
        dpre = (dactive.astype(jnp.float32) * gelu_slope(preact)).astype(jnp.bfloat16)
        up_part = jnp.einsum('ijc,ijf->cf', normed.astype(jnp.float32), dpre.astype(jnp.float32))
        dnorm = jnp.einsum('ijf,cf->ijc', dpre.astype(jnp.float32), up_f)
        gain_part = lax.optimization_barrier(jnp.sum(dnorm * scaled, axis=(0, 1)))
        dscaled = dnorm * norm_gain
        dhidden = (inverse * (dscaled - scaled * lax.optimization_barrier(jnp.mean(dscaled * scaled, axis=-1, keepdims=True)))).astype(jnp.bfloat16)
        disco_part = jnp.einsum('kijc,ijd->kcd', filtered.astype(jnp.float32), dhidden.astype(jnp.float32))
        dfilt = jnp.einsum('ijd,kcd->kijc', dhidden.astype(jnp.float32), disco_f).astype(jnp.bfloat16)
        return (adjoint(dfilt, taps), disco_part, up_part, down_part, gain_part)
    results = lax.map(backward, (dgrad,) + tuple(saved[1:]))
    grad_input = (dgrad.astype(jnp.float32) + results[0]).astype(jnp.bfloat16)
    factor = 1.0 / math.sqrt(MEMBERS * LAT * LON)
    grad_disco = lax.optimization_barrier(jnp.sum(results[1], axis=0)) * factor
    grad_up = lax.optimization_barrier(jnp.sum(results[2], axis=0)) * factor
    grad_down = lax.optimization_barrier(jnp.sum(results[3], axis=0)) * factor
    grad_gain = lax.optimization_barrier(jnp.sum(results[4], axis=0)) * factor
    return (grad_input, grad_disco, grad_up, grad_down, grad_gain)
```

```python
import functools
import math

import jax
import jax.numpy as jnp
from jax import lax
from jax.experimental import pallas as pl
from jax.experimental.pallas import tpu as pltpu
from jax.sharding import PartitionSpec as P

MESH = pl.DeviceIdType.MESH
root_two_pi = 0.7978845608028654


def padded_2(block, sides, width):
    for axis, dim in sides:
        count = lax.axis_size(axis)
        forward = [(i, i + 1) for i in range(count - 1)]
        forward.append((count - 1, 0))
        backward = [(target, source) for source, target in forward]
        low = lax.ppermute(
            lax.slice_in_dim(block, block.shape[dim] - width, None, axis=dim), axis, forward
        )
        high = lax.ppermute(lax.slice_in_dim(block, 0, width, axis=dim), axis, backward)
        block = jnp.concatenate([low, block, high], axis=dim)
    return block


def slope_abs(values):
    return values * lax.rsqrt(values * values + 0.01)


def gelu_value(preact):
    return (
        0.5
        * preact
        * (1.0 + jnp.tanh(root_two_pi * (preact + 0.044715 * preact * preact * preact)))
    )


def gelu_slope(preact):
    tangent = jnp.tanh(root_two_pi * (preact + 0.044715 * preact * preact * preact))
    return 0.5 * (1.0 + tangent) + 0.5 * preact * (1.0 - tangent * tangent) * root_two_pi * (
        1.0 + 3.0 * 0.044715 * preact * preact
    )


def masked_taps(filter_taps, lon_offset, lon_width):
    count = filter_taps.shape[3]
    reach = (count - 1) // 2
    offsets = jnp.arange(count, dtype=jnp.int32) - reach
    keep = jnp.abs(offsets[None, :] - lon_offset[:, None]) <= lon_width[:, None]
    return jnp.where(keep[None, :, None, :], filter_taps, jnp.zeros_like(filter_taps))


def band_matrix(taps, local, mirror):
    count = taps.shape[3]
    reach = (count - 1) // 2
    across = jnp.arange(local + 2 * reach, dtype=jnp.int32)[None, :]
    along = jnp.arange(local, dtype=jnp.int32)[:, None]
    if mirror:
        offset = 2 * reach + along - across
    else:
        offset = across - along
    band = jnp.zeros(taps.shape[:3] + offset.shape, taps.dtype)
    for step in range(count):
        band = jnp.where(offset == step, taps[:, :, :, step, None, None], band)
    return band


def sum_kernel(members, halves, part_ref, full_ref, sum_core, sum_ens, from_core, from_ens, from_space, send, recv):
    ens, space = lax.axis_index("ens"), lax.axis_index("space")
    core, half = lax.rem(space, 2), space // 2
    other = space + 1 - 2 * core
    ens_peers = [(lax.rem(ens + d, members), space) for d in range(1, members)]
    space_peers = [(ens, lax.rem(half + d, halves) * 2 + core) for d in range(1, halves)]
    barrier = pltpu.get_barrier_semaphore()
    everyone = [(ens, other)] + ens_peers + space_peers
    for peer in everyone:
        pl.semaphore_signal(barrier, inc=1, device_id=peer, device_id_type=MESH)
    pl.semaphore_wait(barrier, len(everyone))

    def move(src, dst, slot, peer):
        copy = pltpu.make_async_remote_copy(
            src_ref=src,
            dst_ref=dst,
            send_sem=send.at[slot],
            recv_sem=recv.at[slot],
            device_id=peer,
            device_id_type=MESH,
        )
        copy.start()
        return copy

    wide = members * halves
    first_core = core * wide
    copies = [move(part_ref.at[pl.ds((1 - core) * wide, wide)], from_core, 0, (ens, other))]
    for copy in copies:
        copy.wait()

    def add_core(i, carry):
        total = part_ref[first_core + i].astype(jnp.float32) + from_core[i].astype(jnp.float32)
        sum_core[i] = total.astype(jnp.bfloat16)
        return carry

    lax.fori_loop(0, wide, add_core, 0)

    copies = []
    for d in range(1, members):
        peer = ens_peers[d - 1]
        copies.append(move(sum_core.at[pl.ds(peer[0] * halves, halves)], from_ens.at[d - 1], d, peer))
    for copy in copies:
        copy.wait()

    def add_ens(i, carry):
        total = sum_core[ens * halves + i].astype(jnp.float32)
        for d in range(members - 1):
            total = total + from_ens[d, i].astype(jnp.float32)
        sum_ens[i] = total.astype(jnp.bfloat16)
        return carry

    lax.fori_loop(0, halves, add_ens, 0)

    copies = []
    for d in range(1, halves):
        copies.append(
            move(sum_ens.at[lax.rem(half + d, halves)], from_space.at[d - 1], members - 1 + d, space_peers[d - 1])
        )
    for copy in copies:
        copy.wait()
    total = sum_ens[half].astype(jnp.float32)
    for d in range(halves - 1):
        total = total + from_space[d].astype(jnp.float32)
    first_ens = first_core + ens * halves
    full_ref[first_ens + half] = total.astype(jnp.bfloat16)

    back = members + halves - 1
    copies = []
    for d in range(1, halves):
        block = full_ref.at[pl.ds(first_ens + half, 1)]
        copies.append(move(block, block, back + members - 1 + d, space_peers[d - 1]))
    for copy in copies:
        copy.wait()
    copies = []
    for d in range(1, members):
        block = full_ref.at[pl.ds(first_ens, halves)]
        copies.append(move(block, block, back + d, ens_peers[d - 1]))
    for copy in copies:
        copy.wait()
    block = full_ref.at[pl.ds(first_core, wide)]
    move(block, block, back, (ens, other)).wait()


def sum_everywhere(parts):
    members, halves = lax.axis_size("ens"), lax.axis_size("space") // 2
    blocks = 2 * members * halves
    width = parts[0].shape[1]
    rows = sum(part.shape[0] for part in parts)
    each = -(-rows // (blocks * 16)) * 16
    packed = jnp.concatenate(
        [part.astype(jnp.bfloat16) for part in parts]
        + [jnp.zeros((blocks * each - rows, width), jnp.bfloat16)]
    ).reshape(blocks, each, width)
    whole = pl.BlockSpec(memory_space=pltpu.VMEM)
    count = 2 * (members + halves - 1)
    summed = pl.pallas_call(
        functools.partial(sum_kernel, members, halves),
        out_shape=jax.ShapeDtypeStruct(packed.shape, jnp.bfloat16),
        in_specs=[whole],
        out_specs=whole,
        scratch_shapes=[
            pltpu.VMEM((members * halves, each, width), jnp.bfloat16),
            pltpu.VMEM((halves, each, width), jnp.bfloat16),
            pltpu.VMEM((members * halves, each, width), jnp.bfloat16),
            pltpu.VMEM((max(members - 1, 1), halves, each, width), jnp.bfloat16),
            pltpu.VMEM((max(halves - 1, 1), each, width), jnp.bfloat16),
            pltpu.SemaphoreType.DMA((count,)),
            pltpu.SemaphoreType.DMA((count,)),
        ],
        compiler_params=pltpu.CompilerParams(
            collective_id=1, has_side_effects=True, vmem_limit_bytes=24 * 1024 * 1024
        ),
        name="sum_everywhere",
    )(packed).reshape(blocks * each, width)
    result, start = [], 0
    for part in parts:
        result.append(summed[start : start + part.shape[0]].astype(jnp.float32))
        start += part.shape[0]
    return result


def crps_slope(owned, everyone, aimed):
    mine = owned.astype(jnp.float32)
    miss = slope_abs(mine - aimed.astype(jnp.float32))
    spread = jnp.sum(slope_abs(mine[:, None] - everyone.astype(jnp.float32)[None]), axis=1)
    return (miss - spread / (everyone.shape[0] - 1)).astype(jnp.bfloat16)


def body(inputs, target, filter_taps, lon_offset, lon_width, w_disco, w_up, w_down, norm_gain):
    taps = masked_taps(filter_taps, lon_offset, lon_width)
    reach = (taps.shape[3] - 1) // 2
    members_here = inputs.shape[0]
    rows = inputs.shape[1]
    local = inputs.shape[2]
    channels = inputs.shape[3]
    ahead = band_matrix(taps, local, False)
    padded_lon = padded_2(inputs, (("space", 2),), reach)
    padded = jnp.pad(padded_lon, ((0, 0), (1, 1), (0, 0), (0, 0)))
    total = jnp.zeros((taps.shape[0],) + inputs.shape, jnp.float32)
    for shift_row in range(3):
        total = total + jnp.einsum(
            "kijp,mipc->kmijc",
            ahead[:, :, shift_row],
            padded[:, shift_row : shift_row + rows],
            preferred_element_type=jnp.float32,
        )
    filtered = total.astype(jnp.bfloat16)
    hidden = jnp.einsum("kmijc,kcd->mijd", filtered, w_disco, preferred_element_type=jnp.float32)
    inverse = lax.rsqrt(jnp.mean(hidden * hidden, axis=-1, keepdims=True) + 1e-06)
    scaled = hidden * inverse
    normed = (scaled * norm_gain).astype(jnp.bfloat16)
    preact = jnp.einsum("mijc,cf->mijf", normed, w_up, preferred_element_type=jnp.float32)
    active = gelu_value(preact).astype(jnp.bfloat16)
    output = (
        inputs.astype(jnp.float32)
        + jnp.einsum("mijf,fc->mijc", active, w_down, preferred_element_type=jnp.float32)
    ).astype(jnp.bfloat16)
    everyone = lax.all_gather(output, "ens", axis=0, tiled=True)
    dgrad = crps_slope(output, everyone, target[None])
    down_part = jnp.einsum("mijf,mijc->fc", active, dgrad, preferred_element_type=jnp.float32)
    dactive = jnp.einsum("mijc,fc->mijf", dgrad, w_down, preferred_element_type=jnp.float32).astype(
        jnp.bfloat16
    )
    dpre = (dactive.astype(jnp.float32) * gelu_slope(preact)).astype(jnp.bfloat16)
    up_part = jnp.einsum("mijc,mijf->cf", normed, dpre, preferred_element_type=jnp.float32)
    dnorm = jnp.einsum("mijf,cf->mijc", dpre, w_up, preferred_element_type=jnp.float32)
    gain_part = jnp.sum(dnorm * scaled, axis=(0, 1, 2))
    dscaled = dnorm * norm_gain
    dhidden = (
        inverse * (dscaled - scaled * jnp.mean(dscaled * scaled, axis=-1, keepdims=True))
    ).astype(jnp.bfloat16)
    disco_part = jnp.einsum(
        "kmijc,mijd->kcd", filtered, dhidden, preferred_element_type=jnp.float32
    )
    dfilt = jnp.einsum(
        "mijd,kcd->kmijc", dhidden, w_disco, preferred_element_type=jnp.float32
    ).astype(jnp.bfloat16)
    mirrored = band_matrix(taps, local, True)
    beside_all = padded_2(dfilt, (("space", 3),), reach)
    placed = jnp.einsum(
        "kiajp,kmipc->amijc", mirrored, beside_all, preferred_element_type=jnp.float32
    )
    spread_back = placed[1]
    spread_back = spread_back + jnp.pad(placed[0, :, 1:], ((0, 0), (0, 1), (0, 0), (0, 0)))
    spread_back = spread_back + jnp.pad(placed[2, :, :-1], ((0, 0), (1, 0), (0, 0), (0, 0)))
    grad_input = (dgrad.astype(jnp.float32) + spread_back).astype(jnp.bfloat16)
    hidden_units = up_part.shape[1]
    cuts = range(0, hidden_units, channels)
    pieces = [disco_part.reshape(-1, channels)]
    pieces += [up_part[:, cut : cut + channels] for cut in cuts]
    pieces += [down_part, gain_part[None]]
    summed = sum_everywhere(pieces)
    sums = (
        summed[0].reshape(disco_part.shape),
        jnp.concatenate(summed[1:-2], axis=1),
        summed[-2],
        summed[-1][0],
    )
    factor = 1.0 / math.sqrt(
        members_here * lax.axis_size("ens") * rows * local * lax.axis_size("space")
    )
    return (grad_input, sums[0] * factor, sums[1] * factor, sums[2] * factor, sums[3] * factor)


def solution(mesh):
    placed = (
        P("ens", None, "space", None),
        P(None, "space", None),
        P(),
        P(),
        P(),
        P(),
        P(),
        P(),
        P(),
    )
    return jax.shard_map(
        body,
        mesh=mesh,
        in_specs=placed,
        out_specs=(P("ens", None, "space", None), P(), P(), P(), P()),
        check_vma=False,
    )
```

```python
import functools
import math

import jax
import jax.numpy as jnp
from jax import lax
from jax.experimental import pallas as pl
from jax.experimental.pallas import tpu as pltpu
from jax.sharding import PartitionSpec as P

MESH = pl.DeviceIdType.MESH
root_two_pi = 0.7978845608028654


def padded_2(block, sides, width):
    for axis, dim in sides:
        count = lax.axis_size(axis)
        forward = [(i, i + 1) for i in range(count - 1)]
        forward.append((count - 1, 0))
        backward = [(target, source) for source, target in forward]
        low = lax.ppermute(
            lax.slice_in_dim(block, block.shape[dim] - width, None, axis=dim), axis, forward
        )
        high = lax.ppermute(lax.slice_in_dim(block, 0, width, axis=dim), axis, backward)
        block = jnp.concatenate([low, block, high], axis=dim)
    return block


def slope_abs(values):
    return values * lax.rsqrt(values * values + 0.01)


def gelu_value(preact):
    return (
        0.5
        * preact
        * (1.0 + jnp.tanh(root_two_pi * (preact + 0.044715 * preact * preact * preact)))
    )


def gelu_slope(preact):
    tangent = jnp.tanh(root_two_pi * (preact + 0.044715 * preact * preact * preact))
    return 0.5 * (1.0 + tangent) + 0.5 * preact * (1.0 - tangent * tangent) * root_two_pi * (
        1.0 + 3.0 * 0.044715 * preact * preact
    )


def masked_taps(filter_taps, lon_offset, lon_width):
    count = filter_taps.shape[3]
    reach = (count - 1) // 2
    offsets = jnp.arange(count, dtype=jnp.int32) - reach
    keep = jnp.abs(offsets[None, :] - lon_offset[:, None]) <= lon_width[:, None]
    return jnp.where(keep[None, :, None, :], filter_taps, jnp.zeros_like(filter_taps))


def band_matrix(taps, local, mirror):
    count = taps.shape[3]
    reach = (count - 1) // 2
    across = jnp.arange(local + 2 * reach, dtype=jnp.int32)[None, :]
    along = jnp.arange(local, dtype=jnp.int32)[:, None]
    if mirror:
        offset = 2 * reach + along - across
    else:
        offset = across - along
    band = jnp.zeros(taps.shape[:3] + offset.shape, taps.dtype)
    for step in range(count):
        band = jnp.where(offset == step, taps[:, :, :, step, None, None], band)
    return band


def sum_kernel(members, halves, part_ref, full_ref, sum_core, sum_ens, from_core, from_ens, from_space, send, recv):
    ens, space = lax.axis_index("ens"), lax.axis_index("space")
    core, half = lax.rem(space, 2), space // 2
    other = space + 1 - 2 * core
    ens_peers = [(lax.rem(ens + d, members), space) for d in range(1, members)]
    space_peers = [(ens, lax.rem(half + d, halves) * 2 + core) for d in range(1, halves)]
    barrier = pltpu.get_barrier_semaphore()
    everyone = [(ens, other)] + ens_peers + space_peers
    for peer in everyone:
        pl.semaphore_signal(barrier, inc=1, device_id=peer, device_id_type=MESH)
    pl.semaphore_wait(barrier, len(everyone))

    def move(src, dst, slot, peer):
        copy = pltpu.make_async_remote_copy(
            src_ref=src,
            dst_ref=dst,
            send_sem=send.at[slot],
            recv_sem=recv.at[slot],
            device_id=peer,
            device_id_type=MESH,
        )
        copy.start()
        return copy

    wide = members * halves
    first_core = core * wide
    copies = [move(part_ref.at[pl.ds((1 - core) * wide, wide)], from_core, 0, (ens, other))]
    for copy in copies:
        copy.wait()

    def add_core(i, carry):
        total = part_ref[first_core + i].astype(jnp.float32) + from_core[i].astype(jnp.float32)
        sum_core[i] = total.astype(jnp.bfloat16)
        return carry

    lax.fori_loop(0, wide, add_core, 0)

    copies = []
    for d in range(1, members):
        peer = ens_peers[d - 1]
        copies.append(move(sum_core.at[pl.ds(peer[0] * halves, halves)], from_ens.at[d - 1], d, peer))
    for copy in copies:
        copy.wait()

    def add_ens(i, carry):
        total = sum_core[ens * halves + i].astype(jnp.float32)
        for d in range(members - 1):
            total = total + from_ens[d, i].astype(jnp.float32)
        sum_ens[i] = total.astype(jnp.bfloat16)
        return carry

    lax.fori_loop(0, halves, add_ens, 0)

    copies = []
    for d in range(1, halves):
        copies.append(
            move(sum_ens.at[lax.rem(half + d, halves)], from_space.at[d - 1], members - 1 + d, space_peers[d - 1])
        )
    for copy in copies:
        copy.wait()
    total = sum_ens[half].astype(jnp.float32)
    for d in range(halves - 1):
        total = total + from_space[d].astype(jnp.float32)
    first_ens = first_core + ens * halves
    full_ref[first_ens + half] = total.astype(jnp.bfloat16)

    back = members + halves - 1
    copies = []
    for d in range(1, halves):
        block = full_ref.at[pl.ds(first_ens + half, 1)]
        copies.append(move(block, block, back + members - 1 + d, space_peers[d - 1]))
    for copy in copies:
        copy.wait()
    copies = []
    for d in range(1, members):
        block = full_ref.at[pl.ds(first_ens, halves)]
        copies.append(move(block, block, back + d, ens_peers[d - 1]))
    for copy in copies:
        copy.wait()
    block = full_ref.at[pl.ds(first_core, wide)]
    move(block, block, back, (ens, other)).wait()


def sum_everywhere(parts):
    members, halves = lax.axis_size("ens"), lax.axis_size("space") // 2
    blocks = 2 * members * halves
    width = parts[0].shape[1]
    rows = sum(part.shape[0] for part in parts)
    each = -(-rows // (blocks * 16)) * 16
    packed = jnp.concatenate(
        [part.astype(jnp.bfloat16) for part in parts]
        + [jnp.zeros((blocks * each - rows, width), jnp.bfloat16)]
    ).reshape(blocks, each, width)
    whole = pl.BlockSpec(memory_space=pltpu.VMEM)
    count = 2 * (members + halves - 1)
    summed = pl.pallas_call(
        functools.partial(sum_kernel, members, halves),
        out_shape=jax.ShapeDtypeStruct(packed.shape, jnp.bfloat16),
        in_specs=[whole],
        out_specs=whole,
        scratch_shapes=[
            pltpu.VMEM((members * halves, each, width), jnp.bfloat16),
            pltpu.VMEM((halves, each, width), jnp.bfloat16),
            pltpu.VMEM((members * halves, each, width), jnp.bfloat16),
            pltpu.VMEM((max(members - 1, 1), halves, each, width), jnp.bfloat16),
            pltpu.VMEM((max(halves - 1, 1), each, width), jnp.bfloat16),
            pltpu.SemaphoreType.DMA((count,)),
            pltpu.SemaphoreType.DMA((count,)),
        ],
        compiler_params=pltpu.CompilerParams(
            collective_id=1, has_side_effects=True, vmem_limit_bytes=24 * 1024 * 1024
        ),
        cost_estimate=pl.CostEstimate(flops=3 * 10**10, bytes_accessed=2 * 10**6, transcendentals=0),
        name="sum_everywhere",
    )(packed).reshape(blocks * each, width)
    result, start = [], 0
    for part in parts:
        result.append(summed[start : start + part.shape[0]].astype(jnp.float32))
        start += part.shape[0]
    return result


def crps_kernel(devices, groups, mine_ref, aimed_ref, slope_ref, held, back, out_send, out_recv, back_send, back_recv):
    ens, space = lax.axis_index("ens"), lax.axis_index("space")
    here, rows, local, channels = mine_ref.shape
    share = rows // devices
    few = share // groups
    ahead = [(lax.rem(ens + d, devices), space) for d in range(1, devices)]
    behind = [(lax.rem(ens + devices - d, devices), space) for d in range(1, devices)]
    barrier = pltpu.get_barrier_semaphore()
    for peer in ahead:
        pl.semaphore_signal(barrier, inc=1, device_id=peer, device_id_type=MESH)
    pl.semaphore_wait(barrier, devices - 1)

    going = []
    for group in range(groups):
        for d in range(devices - 1):
            copy = pltpu.make_async_remote_copy(
                src_ref=mine_ref.at[:, pl.ds(ahead[d][0] * share + group * few, few)],
                dst_ref=held.at[d, group],
                send_sem=out_send.at[d, group],
                recv_sem=out_recv.at[d, group],
                device_id=ahead[d],
                device_id_type=MESH,
            )
            copy.start()
            going.append(copy)

    tall, wide = 16, 128
    tiles = local // tall
    count = here * devices
    coming = []
    for group in range(groups):
        for d in range(devices - 1):
            going[group * (devices - 1) + d].wait_recv()
        first = ens * share + group * few

        def tile(step, carry):
            row = step // tiles
            lon = pl.ds(pl.multiple_of(lax.rem(step, tiles) * tall, tall), tall)
            for cut in range(0, channels, wide):
                part = slice(cut, cut + wide)
                values = [mine_ref[m, first + row, lon, part].astype(jnp.float32) for m in range(here)]
                for d in range(devices - 1):
                    values += [held[d, group, m, row, lon, part].astype(jnp.float32) for m in range(here)]
                spread = [jnp.zeros((tall, wide), jnp.float32) for _ in range(count)]
                for m in range(count):
                    for n in range(m + 1, count):
                        pair = slope_abs(values[m] - values[n])
                        spread[m] = spread[m] + pair
                        spread[n] = spread[n] - pair
                goal = aimed_ref[first + row, lon, part].astype(jnp.float32)
                for m in range(count):
                    slope = slope_abs(values[m] - goal) - spread[m] * (1.0 / (count - 1))
                    slope = slope.astype(jnp.bfloat16)
                    if m < here:
                        slope_ref[m, first + row, lon, part] = slope
                    else:
                        back[m // here - 1, group, m % here, row, lon, part] = slope
            return carry

        lax.fori_loop(0, few * tiles, tile, 0)
        for d in range(devices - 1):
            copy = pltpu.make_async_remote_copy(
                src_ref=back.at[d, group],
                dst_ref=slope_ref.at[:, pl.ds(first, few)],
                send_sem=back_send.at[d, group],
                recv_sem=back_recv.at[d, group],
                device_id=behind[d],
                device_id_type=MESH,
            )
            copy.start()
            coming.append((copy, d, group))
    for copy in going:
        copy.wait_send()
    for copy, d, group in coming:
        copy.wait_send()
        copy.wait_recv()


def crps_slope(owned, aimed):
    devices = lax.axis_size("ens")
    here, rows, local, channels = owned.shape
    share = rows // devices
    groups = 2 if share % 2 == 0 else 1
    slots = (devices - 1, groups)
    whole = pl.BlockSpec(memory_space=pltpu.VMEM)
    block = slots + (here, share // groups, local, channels)
    return pl.pallas_call(
        functools.partial(crps_kernel, devices, groups),
        out_shape=jax.ShapeDtypeStruct(owned.shape, jnp.bfloat16),
        in_specs=[whole, whole],
        out_specs=whole,
        scratch_shapes=[pltpu.VMEM(block, jnp.bfloat16)] * 2 + [pltpu.SemaphoreType.DMA(slots)] * 4,
        compiler_params=pltpu.CompilerParams(
            collective_id=2, has_side_effects=True, vmem_limit_bytes=24 * 1024 * 1024
        ),
        name="crps_slope",
    )(owned, aimed)


def body(inputs, target, filter_taps, lon_offset, lon_width, w_disco, w_up, w_down, norm_gain):
    taps = masked_taps(filter_taps, lon_offset, lon_width)
    reach = (taps.shape[3] - 1) // 2
    members_here = inputs.shape[0]
    rows = inputs.shape[1]
    local = inputs.shape[2]
    channels = inputs.shape[3]
    ahead = band_matrix(taps, local, False)
    padded_lon = padded_2(inputs, (("space", 2),), reach)
    padded = jnp.pad(padded_lon, ((0, 0), (1, 1), (0, 0), (0, 0)))
    total = jnp.zeros((taps.shape[0],) + inputs.shape, jnp.float32)
    for shift_row in range(3):
        total = total + jnp.einsum(
            "kijp,mipc->kmijc",
            ahead[:, :, shift_row],
            padded[:, shift_row : shift_row + rows],
            preferred_element_type=jnp.float32,
        )
    filtered = total.astype(jnp.bfloat16)
    hidden = jnp.einsum("kmijc,kcd->mijd", filtered, w_disco, preferred_element_type=jnp.float32)
    inverse = lax.rsqrt(jnp.mean(hidden * hidden, axis=-1, keepdims=True) + 1e-06)
    scaled = hidden * inverse
    normed = (scaled * norm_gain).astype(jnp.bfloat16)
    preact = jnp.einsum("mijc,cf->mijf", normed, w_up, preferred_element_type=jnp.float32)
    active = gelu_value(preact).astype(jnp.bfloat16)
    output = (
        inputs.astype(jnp.float32)
        + jnp.einsum("mijf,fc->mijc", active, w_down, preferred_element_type=jnp.float32)
    ).astype(jnp.bfloat16)
    dgrad = crps_slope(output, target)
    down_part = jnp.einsum("mijf,mijc->fc", active, dgrad, preferred_element_type=jnp.float32)
    dactive = jnp.einsum("mijc,fc->mijf", dgrad, w_down, preferred_element_type=jnp.float32).astype(
        jnp.bfloat16
    )
    dpre = (dactive.astype(jnp.float32) * gelu_slope(preact)).astype(jnp.bfloat16)
    up_part = jnp.einsum("mijc,mijf->cf", normed, dpre, preferred_element_type=jnp.float32)
    dnorm = jnp.einsum("mijf,cf->mijc", dpre, w_up, preferred_element_type=jnp.float32)
    gain_part = jnp.sum(dnorm * scaled, axis=(0, 1, 2))
    dscaled = dnorm * norm_gain
    dhidden = (
        inverse * (dscaled - scaled * jnp.mean(dscaled * scaled, axis=-1, keepdims=True))
    ).astype(jnp.bfloat16)
    disco_part = jnp.einsum(
        "kmijc,mijd->kcd", filtered, dhidden, preferred_element_type=jnp.float32
    )
    dfilt = jnp.einsum(
        "mijd,kcd->kmijc", dhidden, w_disco, preferred_element_type=jnp.float32
    ).astype(jnp.bfloat16)
    mirrored = band_matrix(taps, local, True)
    beside_all = padded_2(dfilt, (("space", 3),), reach)
    placed = [
        jnp.einsum(
            "kijp,kmipc->mijc",
            mirrored[:, :, shift_row],
            beside_all,
            preferred_element_type=jnp.float32,
        )
        for shift_row in range(3)
    ]
    spread_back = placed[1]
    spread_back = spread_back + jnp.pad(placed[0][:, 1:], ((0, 0), (0, 1), (0, 0), (0, 0)))
    spread_back = spread_back + jnp.pad(placed[2][:, :-1], ((0, 0), (1, 0), (0, 0), (0, 0)))
    grad_input = (dgrad.astype(jnp.float32) + spread_back).astype(jnp.bfloat16)
    hidden_units = up_part.shape[1]
    cuts = range(0, hidden_units, channels)
    pieces = [disco_part.reshape(-1, channels)]
    pieces += [up_part[:, cut : cut + channels] for cut in cuts]
    pieces += [down_part, gain_part[None]]
    summed = sum_everywhere(pieces)
    sums = (
        summed[0].reshape(disco_part.shape),
        jnp.concatenate(summed[1:-2], axis=1),
        summed[-2],
        summed[-1][0],
    )
    factor = 1.0 / math.sqrt(
        members_here * lax.axis_size("ens") * rows * local * lax.axis_size("space")
    )
    return (grad_input, sums[0] * factor, sums[1] * factor, sums[2] * factor, sums[3] * factor)


def solution(mesh):
    placed = (
        P("ens", None, "space", None),
        P(None, "space", None),
        P(),
        P(),
        P(),
        P(),
        P(),
        P(),
        P(),
    )
    return jax.shard_map(
        body,
        mesh=mesh,
        in_specs=placed,
        out_specs=(P("ens", None, "space", None), P(), P(), P(), P()),
        check_vma=False,
    )
```

```python
import functools
import math

import jax
import jax.numpy as jnp
from jax import lax
from jax.experimental import pallas as pl
from jax.experimental.pallas import tpu as pltpu
from jax.sharding import PartitionSpec as P

MESH = pl.DeviceIdType.MESH
root_two_pi = 0.7978845608028654


def padded_2(block, sides, width):
    for axis, dim in sides:
        count = lax.axis_size(axis)
        forward = [(i, i + 1) for i in range(count - 1)]
        forward.append((count - 1, 0))
        backward = [(target, source) for source, target in forward]
        low = lax.ppermute(
            lax.slice_in_dim(block, block.shape[dim] - width, None, axis=dim), axis, forward
        )
        high = lax.ppermute(lax.slice_in_dim(block, 0, width, axis=dim), axis, backward)
        block = jnp.concatenate([low, block, high], axis=dim)
    return block


def slope_abs(values):
    return values * lax.rsqrt(values * values + 0.01)


def gelu_value(preact):
    return (
        0.5
        * preact
        * (1.0 + jnp.tanh(root_two_pi * (preact + 0.044715 * preact * preact * preact)))
    )


def gelu_slope(preact):
    tangent = jnp.tanh(root_two_pi * (preact + 0.044715 * preact * preact * preact))
    return 0.5 * (1.0 + tangent) + 0.5 * preact * (1.0 - tangent * tangent) * root_two_pi * (
        1.0 + 3.0 * 0.044715 * preact * preact
    )


def masked_taps(filter_taps, lon_offset, lon_width):
    count = filter_taps.shape[3]
    reach = (count - 1) // 2
    offsets = jnp.arange(count, dtype=jnp.int32) - reach
    keep = jnp.abs(offsets[None, :] - lon_offset[:, None]) <= lon_width[:, None]
    return jnp.where(keep[None, :, None, :], filter_taps, jnp.zeros_like(filter_taps))


def band_matrix(taps, local, mirror):
    count = taps.shape[3]
    reach = (count - 1) // 2
    across = jnp.arange(local + 2 * reach, dtype=jnp.int32)[None, :]
    along = jnp.arange(local, dtype=jnp.int32)[:, None]
    if mirror:
        offset = 2 * reach + along - across
    else:
        offset = across - along
    band = jnp.zeros(taps.shape[:3] + offset.shape, taps.dtype)
    for step in range(count):
        band = jnp.where(offset == step, taps[:, :, :, step, None, None], band)
    return band


def sum_kernel(members, halves, part_ref, edge_ref, full_ref, beside_ref, sum_core, sum_ens, from_core, from_ens, from_space, send, recv):
    ens, space = lax.axis_index("ens"), lax.axis_index("space")
    core, half = lax.rem(space, 2), space // 2
    other = space + 1 - 2 * core
    ens_peers = [(lax.rem(ens + d, members), space) for d in range(1, members)]
    space_peers = [(ens, lax.rem(half + d, halves) * 2 + core) for d in range(1, halves)]
    barrier = pltpu.get_barrier_semaphore()
    right = (ens, lax.rem(space + 1, 2 * halves))
    left = (ens, lax.rem(space + 2 * halves - 1, 2 * halves))
    everyone = [(ens, other), right, left] + ens_peers + space_peers
    for peer in everyone:
        pl.semaphore_signal(barrier, inc=1, device_id=peer, device_id_type=MESH)
    pl.semaphore_wait(barrier, len(everyone))

    def move(src, dst, slot, peer):
        copy = pltpu.make_async_remote_copy(
            src_ref=src,
            dst_ref=dst,
            send_sem=send.at[slot],
            recv_sem=recv.at[slot],
            device_id=peer,
            device_id_type=MESH,
        )
        copy.start()
        return copy

    sides = 2 * (members + halves - 1)
    edges = [
        move(edge_ref.at[0], beside_ref.at[0], sides, right),
        move(edge_ref.at[1], beside_ref.at[1], sides + 1, left),
    ]
    wide = members * halves
    first_core = core * wide
    copies = [move(part_ref.at[pl.ds((1 - core) * wide, wide)], from_core, 0, (ens, other))]
    for copy in copies:
        copy.wait()

    def add_core(i, carry):
        total = part_ref[first_core + i].astype(jnp.float32) + from_core[i].astype(jnp.float32)
        sum_core[i] = total.astype(jnp.bfloat16)
        return carry

    lax.fori_loop(0, wide, add_core, 0)

    copies = []
    for d in range(1, members):
        peer = ens_peers[d - 1]
        copies.append(move(sum_core.at[pl.ds(peer[0] * halves, halves)], from_ens.at[d - 1], d, peer))
    for copy in copies:
        copy.wait()

    def add_ens(i, carry):
        total = sum_core[ens * halves + i].astype(jnp.float32)
        for d in range(members - 1):
            total = total + from_ens[d, i].astype(jnp.float32)
        sum_ens[i] = total.astype(jnp.bfloat16)
        return carry

    lax.fori_loop(0, halves, add_ens, 0)

    copies = []
    for d in range(1, halves):
        copies.append(
            move(sum_ens.at[lax.rem(half + d, halves)], from_space.at[d - 1], members - 1 + d, space_peers[d - 1])
        )
    for copy in copies:
        copy.wait()
    total = sum_ens[half].astype(jnp.float32)
    for d in range(halves - 1):
        total = total + from_space[d].astype(jnp.float32)
    first_ens = first_core + ens * halves
    full_ref[first_ens + half] = total.astype(jnp.bfloat16)

    back = members + halves - 1
    copies = []
    for d in range(1, halves):
        block = full_ref.at[pl.ds(first_ens + half, 1)]
        copies.append(move(block, block, back + members - 1 + d, space_peers[d - 1]))
    for copy in copies:
        copy.wait()
    copies = []
    for d in range(1, members):
        block = full_ref.at[pl.ds(first_ens, halves)]
        copies.append(move(block, block, back + d, ens_peers[d - 1]))
    for copy in copies:
        copy.wait()
    block = full_ref.at[pl.ds(first_core, wide)]
    move(block, block, back, (ens, other)).wait()
    for copy in edges:
        copy.wait()


def sum_everywhere(parts, edges):
    members, halves = lax.axis_size("ens"), lax.axis_size("space") // 2
    blocks = 2 * members * halves
    width = parts[0].shape[1]
    rows = sum(part.shape[0] for part in parts)
    each = -(-rows // (blocks * 16)) * 16
    packed = jnp.concatenate(
        [part.astype(jnp.bfloat16) for part in parts]
        + [jnp.zeros((blocks * each - rows, width), jnp.bfloat16)]
    ).reshape(blocks, each, width)
    whole = pl.BlockSpec(memory_space=pltpu.VMEM)
    count = 2 * (members + halves - 1) + 2
    summed, beside = pl.pallas_call(
        functools.partial(sum_kernel, members, halves),
        out_shape=[
            jax.ShapeDtypeStruct(packed.shape, jnp.bfloat16),
            jax.ShapeDtypeStruct(edges.shape, jnp.bfloat16),
        ],
        in_specs=[whole, whole],
        out_specs=[whole, whole],
        scratch_shapes=[
            pltpu.VMEM((members * halves, each, width), jnp.bfloat16),
            pltpu.VMEM((halves, each, width), jnp.bfloat16),
            pltpu.VMEM((members * halves, each, width), jnp.bfloat16),
            pltpu.VMEM((max(members - 1, 1), halves, each, width), jnp.bfloat16),
            pltpu.VMEM((max(halves - 1, 1), each, width), jnp.bfloat16),
            pltpu.SemaphoreType.DMA((count,)),
            pltpu.SemaphoreType.DMA((count,)),
        ],
        compiler_params=pltpu.CompilerParams(
            collective_id=1, has_side_effects=True, vmem_limit_bytes=24 * 1024 * 1024
        ),
        cost_estimate=pl.CostEstimate(flops=3 * 10**10, bytes_accessed=2 * 10**6, transcendentals=0),
        name="sum_everywhere",
    )(packed, edges)
    summed = summed.reshape(blocks * each, width)
    result, start = [], 0
    for part in parts:
        result.append(summed[start : start + part.shape[0]].astype(jnp.float32))
        start += part.shape[0]
    return result, beside


def crps_kernel(devices, groups, mine_ref, aimed_ref, slope_ref, held, back, out_send, out_recv, back_send, back_recv):
    ens, space = lax.axis_index("ens"), lax.axis_index("space")
    here, rows, local, channels = mine_ref.shape
    share = rows // devices
    few = share // groups
    ahead = [(lax.rem(ens + d, devices), space) for d in range(1, devices)]
    behind = [(lax.rem(ens + devices - d, devices), space) for d in range(1, devices)]
    barrier = pltpu.get_barrier_semaphore()
    for peer in ahead:
        pl.semaphore_signal(barrier, inc=1, device_id=peer, device_id_type=MESH)
    pl.semaphore_wait(barrier, devices - 1)

    going = []
    for group in range(groups):
        for d in range(devices - 1):
            copy = pltpu.make_async_remote_copy(
                src_ref=mine_ref.at[:, pl.ds(ahead[d][0] * share + group * few, few)],
                dst_ref=held.at[d, group],
                send_sem=out_send.at[d, group],
                recv_sem=out_recv.at[d, group],
                device_id=ahead[d],
                device_id_type=MESH,
            )
            copy.start()
            going.append(copy)

    tall, wide = 16, 128
    tiles = local // tall
    count = here * devices
    coming = []
    for group in range(groups):
        for d in range(devices - 1):
            going[group * (devices - 1) + d].wait_recv()
        first = ens * share + group * few

        def tile(step, carry):
            row = step // tiles
            lon = pl.ds(pl.multiple_of(lax.rem(step, tiles) * tall, tall), tall)
            for cut in range(0, channels, wide):
                part = slice(cut, cut + wide)
                values = [mine_ref[m, first + row, lon, part].astype(jnp.float32) for m in range(here)]
                for d in range(devices - 1):
                    values += [held[d, group, m, row, lon, part].astype(jnp.float32) for m in range(here)]
                spread = [jnp.zeros((tall, wide), jnp.float32) for _ in range(count)]
                for m in range(count):
                    for n in range(m + 1, count):
                        pair = slope_abs(values[m] - values[n])
                        spread[m] = spread[m] + pair
                        spread[n] = spread[n] - pair
                goal = aimed_ref[first + row, lon, part].astype(jnp.float32)
                for m in range(count):
                    slope = slope_abs(values[m] - goal) - spread[m] * (1.0 / (count - 1))
                    slope = slope.astype(jnp.bfloat16)
                    if m < here:
                        slope_ref[m, first + row, lon, part] = slope
                    else:
                        back[m // here - 1, group, m % here, row, lon, part] = slope
            return carry

        lax.fori_loop(0, few * tiles, tile, 0)
        for d in range(devices - 1):
            copy = pltpu.make_async_remote_copy(
                src_ref=back.at[d, group],
                dst_ref=slope_ref.at[:, pl.ds(first, few)],
                send_sem=back_send.at[d, group],
                recv_sem=back_recv.at[d, group],
                device_id=behind[d],
                device_id_type=MESH,
            )
            copy.start()
            coming.append((copy, d, group))
    for copy in going:
        copy.wait_send()
    for copy, d, group in coming:
        copy.wait_send()
        copy.wait_recv()


def crps_slope(owned, aimed):
    devices = lax.axis_size("ens")
    here, rows, local, channels = owned.shape
    share = rows // devices
    groups = 2 if share % 2 == 0 else 1
    slots = (devices - 1, groups)
    whole = pl.BlockSpec(memory_space=pltpu.VMEM)
    block = slots + (here, share // groups, local, channels)
    return pl.pallas_call(
        functools.partial(crps_kernel, devices, groups),
        out_shape=jax.ShapeDtypeStruct(owned.shape, jnp.bfloat16),
        in_specs=[whole, whole],
        out_specs=whole,
        scratch_shapes=[pltpu.VMEM(block, jnp.bfloat16)] * 2 + [pltpu.SemaphoreType.DMA(slots)] * 4,
        compiler_params=pltpu.CompilerParams(
            collective_id=2, has_side_effects=True, vmem_limit_bytes=24 * 1024 * 1024
        ),
        name="crps_slope",
    )(owned, aimed)


def body(inputs, target, filter_taps, lon_offset, lon_width, w_disco, w_up, w_down, norm_gain):
    taps = masked_taps(filter_taps, lon_offset, lon_width)
    reach = (taps.shape[3] - 1) // 2
    members_here = inputs.shape[0]
    rows = inputs.shape[1]
    local = inputs.shape[2]
    channels = inputs.shape[3]
    ahead = band_matrix(taps, local, False)
    padded_lon = padded_2(inputs, (("space", 2),), reach)
    padded = jnp.pad(padded_lon, ((0, 0), (1, 1), (0, 0), (0, 0)))
    total = jnp.zeros((taps.shape[0],) + inputs.shape, jnp.float32)
    for shift_row in range(3):
        total = total + jnp.einsum(
            "kijp,mipc->kmijc",
            ahead[:, :, shift_row],
            padded[:, shift_row : shift_row + rows],
            preferred_element_type=jnp.float32,
        )
    filtered = total.astype(jnp.bfloat16)
    hidden = jnp.einsum("kmijc,kcd->mijd", filtered, w_disco, preferred_element_type=jnp.float32)
    inverse = lax.rsqrt(jnp.mean(hidden * hidden, axis=-1, keepdims=True) + 1e-06)
    scaled = hidden * inverse
    normed = (scaled * norm_gain).astype(jnp.bfloat16)
    preact = jnp.einsum("mijc,cf->mijf", normed, w_up, preferred_element_type=jnp.float32)
    active = gelu_value(preact).astype(jnp.bfloat16)
    output = (
        inputs.astype(jnp.float32)
        + jnp.einsum("mijf,fc->mijc", active, w_down, preferred_element_type=jnp.float32)
    ).astype(jnp.bfloat16)
    dgrad = crps_slope(output, target)
    down_part = jnp.einsum("mijf,mijc->fc", active, dgrad, preferred_element_type=jnp.float32)
    dactive = jnp.einsum("mijc,fc->mijf", dgrad, w_down, preferred_element_type=jnp.float32).astype(
        jnp.bfloat16
    )
    dpre = (dactive.astype(jnp.float32) * gelu_slope(preact)).astype(jnp.bfloat16)
    up_part = jnp.einsum("mijc,mijf->cf", normed, dpre, preferred_element_type=jnp.float32)
    dnorm = jnp.einsum("mijf,cf->mijc", dpre, w_up, preferred_element_type=jnp.float32)
    gain_part = jnp.sum(dnorm * scaled, axis=(0, 1, 2))
    dscaled = dnorm * norm_gain
    dhidden = (
        inverse * (dscaled - scaled * jnp.mean(dscaled * scaled, axis=-1, keepdims=True))
    ).astype(jnp.bfloat16)
    disco_part = jnp.einsum(
        "kmijc,mijd->kcd", filtered, dhidden, preferred_element_type=jnp.float32
    )
    dfilt = jnp.einsum(
        "mijd,kcd->kmijc", dhidden, w_disco, preferred_element_type=jnp.float32
    ).astype(jnp.bfloat16)
    hidden_units = up_part.shape[1]
    cuts = range(0, hidden_units, channels)
    pieces = [disco_part.reshape(-1, channels)]
    pieces += [up_part[:, cut : cut + channels] for cut in cuts]
    pieces += [down_part, gain_part[None]]
    edges = jnp.stack([dfilt[:, :, :, local - reach :], dfilt[:, :, :, :reach]])
    summed, beside = sum_everywhere(pieces, edges.reshape(2, -1, channels))
    beside = beside.reshape(edges.shape)
    beside_all = jnp.concatenate([beside[0], dfilt, beside[1]], axis=3)
    sums = (
        summed[0].reshape(disco_part.shape),
        jnp.concatenate(summed[1:-2], axis=1),
        summed[-2],
        summed[-1][0],
    )
    mirrored = band_matrix(taps, local, True)
    placed = [
        jnp.einsum(
            "kijp,kmipc->mijc",
            mirrored[:, :, shift_row],
            beside_all,
            preferred_element_type=jnp.float32,
        )
        for shift_row in range(3)
    ]
    spread_back = placed[1]
    spread_back = spread_back + jnp.pad(placed[0][:, 1:], ((0, 0), (0, 1), (0, 0), (0, 0)))
    spread_back = spread_back + jnp.pad(placed[2][:, :-1], ((0, 0), (1, 0), (0, 0), (0, 0)))
    grad_input = (dgrad.astype(jnp.float32) + spread_back).astype(jnp.bfloat16)
    factor = 1.0 / math.sqrt(
        members_here * lax.axis_size("ens") * rows * local * lax.axis_size("space")
    )
    return (grad_input, sums[0] * factor, sums[1] * factor, sums[2] * factor, sums[3] * factor)


def solution(mesh):
    placed = (
        P("ens", None, "space", None),
        P(None, "space", None),
        P(),
        P(),
        P(),
        P(),
        P(),
        P(),
        P(),
    )
    return jax.shard_map(
        body,
        mesh=mesh,
        in_specs=placed,
        out_specs=(P("ens", None, "space", None), P(), P(), P(), P()),
        check_vma=False,
    )
```

```python
import functools
import math

import jax
import jax.numpy as jnp
from jax import lax
from jax.experimental import pallas as pl
from jax.experimental.pallas import tpu as pltpu
from jax.sharding import PartitionSpec as P

MESH = pl.DeviceIdType.MESH
root_two_pi = 0.7978845608028654


def padded_2(block, sides, width):
    for axis, dim in sides:
        count = lax.axis_size(axis)
        forward = [(i, i + 1) for i in range(count - 1)]
        forward.append((count - 1, 0))
        backward = [(target, source) for source, target in forward]
        low = lax.ppermute(
            lax.slice_in_dim(block, block.shape[dim] - width, None, axis=dim), axis, forward
        )
        high = lax.ppermute(lax.slice_in_dim(block, 0, width, axis=dim), axis, backward)
        block = jnp.concatenate([low, block, high], axis=dim)
    return block


def slope_abs(values):
    return values * lax.rsqrt(values * values + 0.01)


def gelu_value(preact):
    return (
        0.5
        * preact
        * (1.0 + jnp.tanh(root_two_pi * (preact + 0.044715 * preact * preact * preact)))
    )


def gelu_slope(preact):
    tangent = jnp.tanh(root_two_pi * (preact + 0.044715 * preact * preact * preact))
    return 0.5 * (1.0 + tangent) + 0.5 * preact * (1.0 - tangent * tangent) * root_two_pi * (
        1.0 + 3.0 * 0.044715 * preact * preact
    )


def masked_taps(filter_taps, lon_offset, lon_width):
    count = filter_taps.shape[3]
    reach = (count - 1) // 2
    offsets = jnp.arange(count, dtype=jnp.int32) - reach
    keep = jnp.abs(offsets[None, :] - lon_offset[:, None]) <= lon_width[:, None]
    return jnp.where(keep[None, :, None, :], filter_taps, jnp.zeros_like(filter_taps))


def band_matrix(taps, local, mirror):
    count = taps.shape[3]
    reach = (count - 1) // 2
    across = jnp.arange(local + 2 * reach, dtype=jnp.int32)[None, :]
    along = jnp.arange(local, dtype=jnp.int32)[:, None]
    if mirror:
        offset = 2 * reach + along - across
    else:
        offset = across - along
    band = jnp.zeros(taps.shape[:3] + offset.shape, taps.dtype)
    for step in range(count):
        band = jnp.where(offset == step, taps[:, :, :, step, None, None], band)
    return band


def sum_kernel(members, halves, part_ref, edge_ref, full_ref, beside_ref, sum_core, sum_ens, from_core, from_ens, from_space, send, recv):
    ens, space = lax.axis_index("ens"), lax.axis_index("space")
    core, half = lax.rem(space, 2), space // 2
    other = space + 1 - 2 * core
    ens_peers = [(lax.rem(ens + d, members), space) for d in range(1, members)]
    space_peers = [(ens, lax.rem(half + d, halves) * 2 + core) for d in range(1, halves)]
    barrier = pltpu.get_barrier_semaphore()
    right = (ens, lax.rem(space + 1, 2 * halves))
    left = (ens, lax.rem(space + 2 * halves - 1, 2 * halves))
    everyone = [(ens, other), right, left] + ens_peers + space_peers
    for peer in everyone:
        pl.semaphore_signal(barrier, inc=1, device_id=peer, device_id_type=MESH)
    pl.semaphore_wait(barrier, len(everyone))

    def move(src, dst, slot, peer):
        copy = pltpu.make_async_remote_copy(
            src_ref=src,
            dst_ref=dst,
            send_sem=send.at[slot],
            recv_sem=recv.at[slot],
            device_id=peer,
            device_id_type=MESH,
        )
        copy.start()
        return copy

    sides = 2 * (members + halves - 1)
    edges = [
        move(edge_ref.at[0], beside_ref.at[0], sides, right),
        move(edge_ref.at[1], beside_ref.at[1], sides + 1, left),
    ]
    wide = members * halves
    first_core = core * wide
    copies = [move(part_ref.at[pl.ds((1 - core) * wide, wide)], from_core, 0, (ens, other))]
    for copy in copies:
        copy.wait()

    def add_core(i, carry):
        total = part_ref[first_core + i].astype(jnp.float32) + from_core[i].astype(jnp.float32)
        sum_core[i] = total.astype(jnp.bfloat16)
        return carry

    lax.fori_loop(0, wide, add_core, 0)

    copies = []
    for d in range(1, members):
        peer = ens_peers[d - 1]
        copies.append(move(sum_core.at[pl.ds(peer[0] * halves, halves)], from_ens.at[d - 1], d, peer))
    for copy in copies:
        copy.wait()

    def add_ens(i, carry):
        total = sum_core[ens * halves + i].astype(jnp.float32)
        for d in range(members - 1):
            total = total + from_ens[d, i].astype(jnp.float32)
        sum_ens[i] = total.astype(jnp.bfloat16)
        return carry

    lax.fori_loop(0, halves, add_ens, 0)

    copies = []
    for d in range(1, halves):
        copies.append(
            move(sum_ens.at[lax.rem(half + d, halves)], from_space.at[d - 1], members - 1 + d, space_peers[d - 1])
        )
    for copy in copies:
        copy.wait()
    total = sum_ens[half].astype(jnp.float32)
    for d in range(halves - 1):
        total = total + from_space[d].astype(jnp.float32)
    first_ens = first_core + ens * halves
    full_ref[first_ens + half] = total.astype(jnp.bfloat16)

    back = members + halves - 1
    copies = []
    for d in range(1, halves):
        block = full_ref.at[pl.ds(first_ens + half, 1)]
        copies.append(move(block, block, back + members - 1 + d, space_peers[d - 1]))
    for copy in copies:
        copy.wait()
    copies = []
    for d in range(1, members):
        block = full_ref.at[pl.ds(first_ens, halves)]
        copies.append(move(block, block, back + d, ens_peers[d - 1]))
    for copy in copies:
        copy.wait()
    block = full_ref.at[pl.ds(first_core, wide)]
    move(block, block, back, (ens, other)).wait()
    for copy in edges:
        copy.wait()


def sum_everywhere(parts, edges):
    members, halves = lax.axis_size("ens"), lax.axis_size("space") // 2
    blocks = 2 * members * halves
    width = parts[0].shape[1]
    rows = sum(part.shape[0] for part in parts)
    each = -(-rows // (blocks * 16)) * 16
    packed = jnp.concatenate(
        [part.astype(jnp.bfloat16) for part in parts]
        + [jnp.zeros((blocks * each - rows, width), jnp.bfloat16)]
    ).reshape(blocks, each, width)
    whole = pl.BlockSpec(memory_space=pltpu.VMEM)
    count = 2 * (members + halves - 1) + 2
    summed, beside = pl.pallas_call(
        functools.partial(sum_kernel, members, halves),
        out_shape=[
            jax.ShapeDtypeStruct(packed.shape, jnp.bfloat16),
            jax.ShapeDtypeStruct(edges.shape, jnp.bfloat16),
        ],
        in_specs=[whole, whole],
        out_specs=[whole, whole],
        scratch_shapes=[
            pltpu.VMEM((members * halves, each, width), jnp.bfloat16),
            pltpu.VMEM((halves, each, width), jnp.bfloat16),
            pltpu.VMEM((members * halves, each, width), jnp.bfloat16),
            pltpu.VMEM((max(members - 1, 1), halves, each, width), jnp.bfloat16),
            pltpu.VMEM((max(halves - 1, 1), each, width), jnp.bfloat16),
            pltpu.SemaphoreType.DMA((count,)),
            pltpu.SemaphoreType.DMA((count,)),
        ],
        compiler_params=pltpu.CompilerParams(
            collective_id=1, has_side_effects=True, vmem_limit_bytes=24 * 1024 * 1024
        ),
        cost_estimate=pl.CostEstimate(flops=3 * 10**10, bytes_accessed=2 * 10**6, transcendentals=0),
        name="sum_everywhere",
    )(packed, edges)
    summed = summed.reshape(blocks * each, width)
    result, start = [], 0
    for part in parts:
        result.append(summed[start : start + part.shape[0]].astype(jnp.float32))
        start += part.shape[0]
    return result, beside


def crps_kernel(devices, groups, mine_ref, aimed_ref, slope_ref, held, back, out_send, out_recv, back_send, back_recv):
    ens, space = lax.axis_index("ens"), lax.axis_index("space")
    here, rows, local, channels = mine_ref.shape
    share = rows // devices
    few = share // groups
    ahead = [(lax.rem(ens + d, devices), space) for d in range(1, devices)]
    behind = [(lax.rem(ens + devices - d, devices), space) for d in range(1, devices)]
    barrier = pltpu.get_barrier_semaphore()
    for peer in ahead:
        pl.semaphore_signal(barrier, inc=1, device_id=peer, device_id_type=MESH)
    pl.semaphore_wait(barrier, devices - 1)

    going = []
    for group in range(groups):
        for d in range(devices - 1):
            copy = pltpu.make_async_remote_copy(
                src_ref=mine_ref.at[:, pl.ds(ahead[d][0] * share + group * few, few)],
                dst_ref=held.at[d, group],
                send_sem=out_send.at[d, group],
                recv_sem=out_recv.at[d, group],
                device_id=ahead[d],
                device_id_type=MESH,
            )
            copy.start()
            going.append(copy)

    tall, wide = 16, 128
    tiles = local // tall
    count = here * devices
    coming = []
    for group in range(groups):
        for d in range(devices - 1):
            going[group * (devices - 1) + d].wait_recv()
        first = ens * share + group * few

        def tile(step, carry):
            row = step // tiles
            lon = pl.ds(pl.multiple_of(lax.rem(step, tiles) * tall, tall), tall)
            for cut in range(0, channels, wide):
                part = slice(cut, cut + wide)
                values = [mine_ref[m, first + row, lon, part].astype(jnp.float32) for m in range(here)]
                for d in range(devices - 1):
                    values += [held[d, group, m, row, lon, part].astype(jnp.float32) for m in range(here)]
                spread = [jnp.zeros((tall, wide), jnp.float32) for _ in range(count)]
                for m in range(count):
                    for n in range(m + 1, count):
                        pair = slope_abs(values[m] - values[n])
                        spread[m] = spread[m] + pair
                        spread[n] = spread[n] - pair
                goal = aimed_ref[first + row, lon, part].astype(jnp.float32)
                for m in range(count):
                    slope = slope_abs(values[m] - goal) - spread[m] * (1.0 / (count - 1))
                    slope = slope.astype(jnp.bfloat16)
                    if m < here:
                        slope_ref[m, first + row, lon, part] = slope
                    else:
                        back[m // here - 1, group, m % here, row, lon, part] = slope
            return carry

        lax.fori_loop(0, few * tiles, tile, 0)
        for d in range(devices - 1):
            copy = pltpu.make_async_remote_copy(
                src_ref=back.at[d, group],
                dst_ref=slope_ref.at[:, pl.ds(first, few)],
                send_sem=back_send.at[d, group],
                recv_sem=back_recv.at[d, group],
                device_id=behind[d],
                device_id_type=MESH,
            )
            copy.start()
            coming.append((copy, d, group))
    for copy in going:
        copy.wait_send()
    for copy, d, group in coming:
        copy.wait_send()
        copy.wait_recv()


def crps_slope(owned, aimed):
    devices = lax.axis_size("ens")
    here, rows, local, channels = owned.shape
    share = rows // devices
    groups = next(g for g in (4, 2, 1) if share % g == 0)
    slots = (devices - 1, groups)
    whole = pl.BlockSpec(memory_space=pltpu.VMEM)
    block = slots + (here, share // groups, local, channels)
    return pl.pallas_call(
        functools.partial(crps_kernel, devices, groups),
        out_shape=jax.ShapeDtypeStruct(owned.shape, jnp.bfloat16),
        in_specs=[whole, whole],
        out_specs=whole,
        scratch_shapes=[pltpu.VMEM(block, jnp.bfloat16)] * 2 + [pltpu.SemaphoreType.DMA(slots)] * 4,
        compiler_params=pltpu.CompilerParams(
            collective_id=2, has_side_effects=True, vmem_limit_bytes=24 * 1024 * 1024
        ),
        name="crps_slope",
    )(owned, aimed)


def body(inputs, target, filter_taps, lon_offset, lon_width, w_disco, w_up, w_down, norm_gain):
    taps = masked_taps(filter_taps, lon_offset, lon_width)
    reach = (taps.shape[3] - 1) // 2
    members_here = inputs.shape[0]
    rows = inputs.shape[1]
    local = inputs.shape[2]
    channels = inputs.shape[3]
    ahead = band_matrix(taps, local, False)
    padded_lon = padded_2(inputs, (("space", 2),), reach)
    padded = jnp.pad(padded_lon, ((0, 0), (1, 1), (0, 0), (0, 0)))
    total = jnp.zeros((taps.shape[0],) + inputs.shape, jnp.float32)
    for shift_row in range(3):
        total = total + jnp.einsum(
            "kijp,mipc->kmijc",
            ahead[:, :, shift_row],
            padded[:, shift_row : shift_row + rows],
            preferred_element_type=jnp.float32,
        )
    filtered = total.astype(jnp.bfloat16)
    hidden = jnp.einsum("kmijc,kcd->mijd", filtered, w_disco, preferred_element_type=jnp.float32)
    inverse = lax.rsqrt(jnp.mean(hidden * hidden, axis=-1, keepdims=True) + 1e-06)
    scaled = hidden * inverse
    normed = (scaled * norm_gain).astype(jnp.bfloat16)
    preact = jnp.einsum("mijc,cf->mijf", normed, w_up, preferred_element_type=jnp.float32)
    active = gelu_value(preact).astype(jnp.bfloat16)
    output = (
        inputs.astype(jnp.float32)
        + jnp.einsum("mijf,fc->mijc", active, w_down, preferred_element_type=jnp.float32)
    ).astype(jnp.bfloat16)
    dgrad = crps_slope(output, target)
    down_part = jnp.einsum("mijf,mijc->fc", active, dgrad, preferred_element_type=jnp.float32)
    dactive = jnp.einsum("mijc,fc->mijf", dgrad, w_down, preferred_element_type=jnp.float32).astype(
        jnp.bfloat16
    )
    dpre = (dactive.astype(jnp.float32) * gelu_slope(preact)).astype(jnp.bfloat16)
    up_part = jnp.einsum("mijc,mijf->cf", normed, dpre, preferred_element_type=jnp.float32)
    dnorm = jnp.einsum("mijf,cf->mijc", dpre, w_up, preferred_element_type=jnp.float32)
    gain_part = jnp.sum(dnorm * scaled, axis=(0, 1, 2))
    dscaled = dnorm * norm_gain
    dhidden = (
        inverse * (dscaled - scaled * jnp.mean(dscaled * scaled, axis=-1, keepdims=True))
    ).astype(jnp.bfloat16)
    disco_part = jnp.einsum(
        "kmijc,mijd->kcd", filtered, dhidden, preferred_element_type=jnp.float32
    )
    dfilt = jnp.einsum(
        "mijd,kcd->kmijc", dhidden, w_disco, preferred_element_type=jnp.float32
    ).astype(jnp.bfloat16)
    hidden_units = up_part.shape[1]
    cuts = range(0, hidden_units, channels)
    pieces = [disco_part.reshape(-1, channels)]
    pieces += [up_part[:, cut : cut + channels] for cut in cuts]
    pieces += [down_part, gain_part[None]]
    edges = jnp.stack([dfilt[:, :, :, local - reach :], dfilt[:, :, :, :reach]])
    summed, beside = sum_everywhere(pieces, edges.reshape(2, -1, channels))
    beside = beside.reshape(edges.shape)
    beside_all = jnp.concatenate([beside[0], dfilt, beside[1]], axis=3)
    sums = (
        summed[0].reshape(disco_part.shape),
        jnp.concatenate(summed[1:-2], axis=1),
        summed[-2],
        summed[-1][0],
    )
    mirrored = band_matrix(taps, local, True)
    placed = [
        jnp.einsum(
            "kijp,kmipc->mijc",
            mirrored[:, :, shift_row],
            beside_all,
            preferred_element_type=jnp.float32,
        )
        for shift_row in range(3)
    ]
    spread_back = placed[1]
    spread_back = spread_back + jnp.pad(placed[0][:, 1:], ((0, 0), (0, 1), (0, 0), (0, 0)))
    spread_back = spread_back + jnp.pad(placed[2][:, :-1], ((0, 0), (1, 0), (0, 0), (0, 0)))
    grad_input = (dgrad.astype(jnp.float32) + spread_back).astype(jnp.bfloat16)
    factor = 1.0 / math.sqrt(
        members_here * lax.axis_size("ens") * rows * local * lax.axis_size("space")
    )
    return (grad_input, sums[0] * factor, sums[1] * factor, sums[2] * factor, sums[3] * factor)


def solution(mesh):
    placed = (
        P("ens", None, "space", None),
        P(None, "space", None),
        P(),
        P(),
        P(),
        P(),
        P(),
        P(),
        P(),
    )
    return jax.shard_map(
        body,
        mesh=mesh,
        in_specs=placed,
        out_specs=(P("ens", None, "space", None), P(), P(), P(), P()),
        check_vma=False,
    )
```

```python
import functools
import math

import jax
import jax.numpy as jnp
from jax import lax
from jax.experimental import pallas as pl
from jax.experimental.pallas import tpu as pltpu
from jax.sharding import PartitionSpec as P

MESH = pl.DeviceIdType.MESH
root_two_pi = 0.7978845608028654


def padded_2(block, sides, width):
    for axis, dim in sides:
        count = lax.axis_size(axis)
        forward = [(i, i + 1) for i in range(count - 1)]
        forward.append((count - 1, 0))
        backward = [(target, source) for source, target in forward]
        low = lax.ppermute(
            lax.slice_in_dim(block, block.shape[dim] - width, None, axis=dim), axis, forward
        )
        high = lax.ppermute(lax.slice_in_dim(block, 0, width, axis=dim), axis, backward)
        block = jnp.concatenate([low, block, high], axis=dim)
    return block


def slope_abs(values):
    return values * lax.rsqrt(values * values + 0.01)


def gelu_value(preact):
    return (
        0.5
        * preact
        * (1.0 + jnp.tanh(root_two_pi * (preact + 0.044715 * preact * preact * preact)))
    )


def gelu_slope(preact):
    tangent = jnp.tanh(root_two_pi * (preact + 0.044715 * preact * preact * preact))
    return 0.5 * (1.0 + tangent) + 0.5 * preact * (1.0 - tangent * tangent) * root_two_pi * (
        1.0 + 3.0 * 0.044715 * preact * preact
    )


def masked_taps(filter_taps, lon_offset, lon_width):
    count = filter_taps.shape[3]
    reach = (count - 1) // 2
    offsets = jnp.arange(count, dtype=jnp.int32) - reach
    keep = jnp.abs(offsets[None, :] - lon_offset[:, None]) <= lon_width[:, None]
    return jnp.where(keep[None, :, None, :], filter_taps, jnp.zeros_like(filter_taps))


def band_matrix(taps, local, mirror):
    count = taps.shape[3]
    reach = (count - 1) // 2
    across = jnp.arange(local + 2 * reach, dtype=jnp.int32)[None, :]
    along = jnp.arange(local, dtype=jnp.int32)[:, None]
    if mirror:
        offset = 2 * reach + along - across
    else:
        offset = across - along
    steps = jnp.arange(count, dtype=jnp.int32)[:, None, None]
    picks = (offset[None] == steps).astype(taps.dtype)
    return jnp.einsum("kiat,tjp->kiajp", taps, picks, preferred_element_type=jnp.float32).astype(
        taps.dtype
    )


def sum_kernel(members, halves, part_ref, edge_ref, full_ref, beside_ref, sum_core, sum_ens, from_core, from_ens, from_space, send, recv):
    ens, space = lax.axis_index("ens"), lax.axis_index("space")
    core, half = lax.rem(space, 2), space // 2
    other = space + 1 - 2 * core
    ens_peers = [(lax.rem(ens + d, members), space) for d in range(1, members)]
    space_peers = [(ens, lax.rem(half + d, halves) * 2 + core) for d in range(1, halves)]
    barrier = pltpu.get_barrier_semaphore()
    right = (ens, lax.rem(space + 1, 2 * halves))
    left = (ens, lax.rem(space + 2 * halves - 1, 2 * halves))
    everyone = [(ens, other), right, left] + ens_peers + space_peers
    for peer in everyone:
        pl.semaphore_signal(barrier, inc=1, device_id=peer, device_id_type=MESH)
    pl.semaphore_wait(barrier, len(everyone))

    def move(src, dst, slot, peer):
        copy = pltpu.make_async_remote_copy(
            src_ref=src,
            dst_ref=dst,
            send_sem=send.at[slot],
            recv_sem=recv.at[slot],
            device_id=peer,
            device_id_type=MESH,
        )
        copy.start()
        return copy

    sides = 2 * (members + halves - 1)
    edges = [
        move(edge_ref.at[0], beside_ref.at[0], sides, right),
        move(edge_ref.at[1], beside_ref.at[1], sides + 1, left),
    ]
    wide = members * halves
    first_core = core * wide
    copies = [move(part_ref.at[pl.ds((1 - core) * wide, wide)], from_core, 0, (ens, other))]
    for copy in copies:
        copy.wait()

    def add_core(i, carry):
        total = part_ref[first_core + i].astype(jnp.float32) + from_core[i].astype(jnp.float32)
        sum_core[i] = total.astype(jnp.bfloat16)
        return carry

    lax.fori_loop(0, wide, add_core, 0)

    copies = []
    for d in range(1, members):
        peer = ens_peers[d - 1]
        copies.append(move(sum_core.at[pl.ds(peer[0] * halves, halves)], from_ens.at[d - 1], d, peer))
    for copy in copies:
        copy.wait()

    def add_ens(i, carry):
        total = sum_core[ens * halves + i].astype(jnp.float32)
        for d in range(members - 1):
            total = total + from_ens[d, i].astype(jnp.float32)
        sum_ens[i] = total.astype(jnp.bfloat16)
        return carry

    lax.fori_loop(0, halves, add_ens, 0)

    copies = []
    for d in range(1, halves):
        copies.append(
            move(sum_ens.at[lax.rem(half + d, halves)], from_space.at[d - 1], members - 1 + d, space_peers[d - 1])
        )
    for copy in copies:
        copy.wait()
    total = sum_ens[half].astype(jnp.float32)
    for d in range(halves - 1):
        total = total + from_space[d].astype(jnp.float32)
    first_ens = first_core + ens * halves
    full_ref[first_ens + half] = total.astype(jnp.bfloat16)

    back = members + halves - 1
    copies = []
    for d in range(1, halves):
        block = full_ref.at[pl.ds(first_ens + half, 1)]
        copies.append(move(block, block, back + members - 1 + d, space_peers[d - 1]))
    for copy in copies:
        copy.wait()
    copies = []
    for d in range(1, members):
        block = full_ref.at[pl.ds(first_ens, halves)]
        copies.append(move(block, block, back + d, ens_peers[d - 1]))
    for copy in copies:
        copy.wait()
    block = full_ref.at[pl.ds(first_core, wide)]
    move(block, block, back, (ens, other)).wait()
    for copy in edges:
        copy.wait()


def sum_everywhere(parts, edges):
    members, halves = lax.axis_size("ens"), lax.axis_size("space") // 2
    blocks = 2 * members * halves
    width = parts[0].shape[1]
    rows = sum(part.shape[0] for part in parts)
    each = -(-rows // (blocks * 16)) * 16
    packed = jnp.concatenate(
        [part.astype(jnp.bfloat16) for part in parts]
        + [jnp.zeros((blocks * each - rows, width), jnp.bfloat16)]
    ).reshape(blocks, each, width)
    whole = pl.BlockSpec(memory_space=pltpu.VMEM)
    count = 2 * (members + halves - 1) + 2
    summed, beside = pl.pallas_call(
        functools.partial(sum_kernel, members, halves),
        out_shape=[
            jax.ShapeDtypeStruct(packed.shape, jnp.bfloat16),
            jax.ShapeDtypeStruct(edges.shape, jnp.bfloat16),
        ],
        in_specs=[whole, whole],
        out_specs=[whole, whole],
        scratch_shapes=[
            pltpu.VMEM((members * halves, each, width), jnp.bfloat16),
            pltpu.VMEM((halves, each, width), jnp.bfloat16),
            pltpu.VMEM((members * halves, each, width), jnp.bfloat16),
            pltpu.VMEM((max(members - 1, 1), halves, each, width), jnp.bfloat16),
            pltpu.VMEM((max(halves - 1, 1), each, width), jnp.bfloat16),
            pltpu.SemaphoreType.DMA((count,)),
            pltpu.SemaphoreType.DMA((count,)),
        ],
        compiler_params=pltpu.CompilerParams(
            collective_id=1, has_side_effects=True, vmem_limit_bytes=24 * 1024 * 1024
        ),
        cost_estimate=pl.CostEstimate(flops=3 * 10**10, bytes_accessed=2 * 10**6, transcendentals=0),
        name="sum_everywhere",
    )(packed, edges)
    summed = summed.reshape(blocks * each, width)
    result, start = [], 0
    for part in parts:
        result.append(summed[start : start + part.shape[0]].astype(jnp.float32))
        start += part.shape[0]
    return result, beside


def crps_kernel(devices, groups, mine_ref, aimed_ref, slope_ref, held, back, out_send, out_recv, back_send, back_recv):
    ens, space = lax.axis_index("ens"), lax.axis_index("space")
    here, rows, local, channels = mine_ref.shape
    share = rows // devices
    few = share // groups
    ahead = [(lax.rem(ens + d, devices), space) for d in range(1, devices)]
    behind = [(lax.rem(ens + devices - d, devices), space) for d in range(1, devices)]
    barrier = pltpu.get_barrier_semaphore()
    for peer in ahead:
        pl.semaphore_signal(barrier, inc=1, device_id=peer, device_id_type=MESH)
    pl.semaphore_wait(barrier, devices - 1)

    going = []
    for group in range(groups):
        for d in range(devices - 1):
            copy = pltpu.make_async_remote_copy(
                src_ref=mine_ref.at[:, pl.ds(ahead[d][0] * share + group * few, few)],
                dst_ref=held.at[d, group],
                send_sem=out_send.at[d, group],
                recv_sem=out_recv.at[d, group],
                device_id=ahead[d],
                device_id_type=MESH,
            )
            copy.start()
            going.append(copy)

    tall, wide = 16, 128
    tiles = local // tall
    count = here * devices
    coming = []
    for group in range(groups):
        for d in range(devices - 1):
            going[group * (devices - 1) + d].wait_recv()
        first = ens * share + group * few

        def tile(step, carry):
            row = step // tiles
            lon = pl.ds(pl.multiple_of(lax.rem(step, tiles) * tall, tall), tall)
            for cut in range(0, channels, wide):
                part = slice(cut, cut + wide)
                values = [mine_ref[m, first + row, lon, part].astype(jnp.float32) for m in range(here)]
                for d in range(devices - 1):
                    values += [held[d, group, m, row, lon, part].astype(jnp.float32) for m in range(here)]
                spread = [jnp.zeros((tall, wide), jnp.float32) for _ in range(count)]
                for m in range(count):
                    for n in range(m + 1, count):
                        pair = slope_abs(values[m] - values[n])
                        spread[m] = spread[m] + pair
                        spread[n] = spread[n] - pair
                goal = aimed_ref[first + row, lon, part].astype(jnp.float32)
                for m in range(count):
                    slope = slope_abs(values[m] - goal) - spread[m] * (1.0 / (count - 1))
                    slope = slope.astype(jnp.bfloat16)
                    if m < here:
                        slope_ref[m, first + row, lon, part] = slope
                    else:
                        back[m // here - 1, group, m % here, row, lon, part] = slope
            return carry

        lax.fori_loop(0, few * tiles, tile, 0)
        for d in range(devices - 1):
            copy = pltpu.make_async_remote_copy(
                src_ref=back.at[d, group],
                dst_ref=slope_ref.at[:, pl.ds(first, few)],
                send_sem=back_send.at[d, group],
                recv_sem=back_recv.at[d, group],
                device_id=behind[d],
                device_id_type=MESH,
            )
            copy.start()
            coming.append((copy, d, group))
    for copy in going:
        copy.wait_send()
    for copy, d, group in coming:
        copy.wait_send()
        copy.wait_recv()


def crps_slope(owned, aimed):
    devices = lax.axis_size("ens")
    here, rows, local, channels = owned.shape
    share = rows // devices
    groups = 2 if share % 2 == 0 else 1
    slots = (devices - 1, groups)
    whole = pl.BlockSpec(memory_space=pltpu.VMEM)
    block = slots + (here, share // groups, local, channels)
    return pl.pallas_call(
        functools.partial(crps_kernel, devices, groups),
        out_shape=jax.ShapeDtypeStruct(owned.shape, jnp.bfloat16),
        in_specs=[whole, whole],
        out_specs=whole,
        scratch_shapes=[pltpu.VMEM(block, jnp.bfloat16)] * 2 + [pltpu.SemaphoreType.DMA(slots)] * 4,
        compiler_params=pltpu.CompilerParams(
            collective_id=2, has_side_effects=True, vmem_limit_bytes=24 * 1024 * 1024
        ),
        name="crps_slope",
    )(owned, aimed)


def body(inputs, target, filter_taps, lon_offset, lon_width, w_disco, w_up, w_down, norm_gain):
    taps = masked_taps(filter_taps, lon_offset, lon_width)
    reach = (taps.shape[3] - 1) // 2
    members_here = inputs.shape[0]
    rows = inputs.shape[1]
    local = inputs.shape[2]
    channels = inputs.shape[3]
    ahead = band_matrix(taps, local, False)
    padded_lon = padded_2(inputs, (("space", 2),), reach)
    padded = jnp.pad(padded_lon, ((0, 0), (1, 1), (0, 0), (0, 0)))
    total = jnp.zeros((taps.shape[0],) + inputs.shape, jnp.float32)
    for shift_row in range(3):
        total = total + jnp.einsum(
            "kijp,mipc->kmijc",
            ahead[:, :, shift_row],
            padded[:, shift_row : shift_row + rows],
            preferred_element_type=jnp.float32,
        )
    filtered = total.astype(jnp.bfloat16)
    hidden = jnp.einsum("kmijc,kcd->mijd", filtered, w_disco, preferred_element_type=jnp.float32)
    inverse = lax.rsqrt(jnp.mean(hidden * hidden, axis=-1, keepdims=True) + 1e-06)
    scaled = hidden * inverse
    normed = (scaled * norm_gain).astype(jnp.bfloat16)
    preact = jnp.einsum("mijc,cf->mijf", normed, w_up, preferred_element_type=jnp.float32)
    active = gelu_value(preact).astype(jnp.bfloat16)
    output = (
        inputs.astype(jnp.float32)
        + jnp.einsum("mijf,fc->mijc", active, w_down, preferred_element_type=jnp.float32)
    ).astype(jnp.bfloat16)
    dgrad = crps_slope(output, target)
    down_part = jnp.einsum("mijf,mijc->fc", active, dgrad, preferred_element_type=jnp.float32)
    dactive = jnp.einsum("mijc,fc->mijf", dgrad, w_down, preferred_element_type=jnp.float32).astype(
        jnp.bfloat16
    )
    dpre = (dactive.astype(jnp.float32) * gelu_slope(preact)).astype(jnp.bfloat16)
    up_part = jnp.einsum("mijc,mijf->cf", normed, dpre, preferred_element_type=jnp.float32)
    dnorm = jnp.einsum("mijf,cf->mijc", dpre, w_up, preferred_element_type=jnp.float32)
    gain_part = jnp.sum(dnorm * scaled, axis=(0, 1, 2))
    dscaled = dnorm * norm_gain
    dhidden = (
        inverse * (dscaled - scaled * jnp.mean(dscaled * scaled, axis=-1, keepdims=True))
    ).astype(jnp.bfloat16)
    disco_part = jnp.einsum(
        "kmijc,mijd->kcd", filtered, dhidden, preferred_element_type=jnp.float32
    )
    dfilt = jnp.einsum(
        "mijd,kcd->kmijc", dhidden, w_disco, preferred_element_type=jnp.float32
    ).astype(jnp.bfloat16)
    hidden_units = up_part.shape[1]
    cuts = range(0, hidden_units, channels)
    pieces = [disco_part.reshape(-1, channels)]
    pieces += [up_part[:, cut : cut + channels] for cut in cuts]
    pieces += [down_part, gain_part[None]]
    edges = jnp.stack([dfilt[:, :, :, local - reach :], dfilt[:, :, :, :reach]])
    summed, beside = sum_everywhere(pieces, edges.reshape(2, -1, channels))
    beside = beside.reshape(edges.shape)
    beside_all = jnp.concatenate([beside[0], dfilt, beside[1]], axis=3)
    sums = (
        summed[0].reshape(disco_part.shape),
        jnp.concatenate(summed[1:-2], axis=1),
        summed[-2],
        summed[-1][0],
    )
    mirrored = band_matrix(taps, local, True)
    placed = [
        jnp.einsum(
            "kijp,kmipc->mijc",
            mirrored[:, :, shift_row],
            beside_all,
            preferred_element_type=jnp.float32,
        )
        for shift_row in range(3)
    ]
    spread_back = placed[1]
    spread_back = spread_back + jnp.pad(placed[0][:, 1:], ((0, 0), (0, 1), (0, 0), (0, 0)))
    spread_back = spread_back + jnp.pad(placed[2][:, :-1], ((0, 0), (1, 0), (0, 0), (0, 0)))
    grad_input = (dgrad.astype(jnp.float32) + spread_back).astype(jnp.bfloat16)
    factor = 1.0 / math.sqrt(
        members_here * lax.axis_size("ens") * rows * local * lax.axis_size("space")
    )
    return (grad_input, sums[0] * factor, sums[1] * factor, sums[2] * factor, sums[3] * factor)


def solution(mesh):
    placed = (
        P("ens", None, "space", None),
        P(None, "space", None),
        P(),
        P(),
        P(),
        P(),
        P(),
        P(),
        P(),
    )
    return jax.shard_map(
        body,
        mesh=mesh,
        in_specs=placed,
        out_specs=(P("ens", None, "space", None), P(), P(), P(), P()),
        check_vma=False,
    )
```
